512 devices in a mesh: span: 8 (over z_hi, core), seq: 16 (over z_lo, y), tensor: 4 (over x).
Axes of the slice: x: 4, y: 4, z: 16 (z_hi: 4, z_lo: 4; z = z_hi * 4 + z_lo), core: 2. Of those that a mesh axis runs over, the one named last changes fastest.
Arguments:
- queries: bfloat16 [8192, 3072], P(('span', 'seq'), 'tensor'), may hold values from -20 to 20
- key_value_pairs: bfloat16 [8192, 2, 512], P(('span', 'seq'), None, 'tensor'), may hold values from -20 to 20
- out_weight: bfloat16 [3072, 3072], P('tensor', 'seq'), may hold values from -0.109375 to 0.109375
- gate_table: float32 [64, 3072], P(None, 'tensor'), may hold values from -4 to 4
- norm_gain: float32 [3072], P('tensor'), may hold values from 0.5 to 1.5
- plan: int32 [8], replicated, may hold values from 0 to 7, each once
- noise_level: int32 [8], replicated, may hold values from 0 to 63
- span_mask: int32 [8, 8, 16], replicated, may hold values from 0 to 1, as said below
Outputs:
- attended: bfloat16 [8192, 3072], P(('span', 'seq'), 'tensor')
The draws below stay inside these ranges and needn't reach their ends.
Inputs may be any that keep to these rules, and one draw needn't show every extreme that they name: `span_mask`: entry [p, q, f] is 1 where q == p and 0 where q > p.
All inputs are finite; a program needn't handle non-finite values.
Results may differ from the reference program's by a relative error of at most 0.018.
Values may be sent and summed in bfloat16 or wider, within the bound.
A program may use at most 64 MiB of HBM per device.

```python
import math
import jax
import jax.numpy as jnp
from jax import lax

D = 3072
QUERY_HEAD_COUNT = 24
KEY_VALUE_HEADS = 4
HEAD_WIDTH = 128
LEVELS = 64
FRAMES = 16
TOKEN_COUNT = 8192
N_SPAN = 8


def draw_queries(key, part):
    key = jax.random.fold_in(key, 11)
    first_factor = jax.random.fold_in(key, 0)
    base = jnp.clip(jax.random.normal(first_factor, (TOKEN_COUNT, QUERY_HEAD_COUNT * HEAD_WIDTH), jnp.float32), -6.0, 6.0)
    return base.astype(jnp.bfloat16)


def draw_key_value_pairs(key, part):
    key = jax.random.fold_in(key, 13)
    first_factor, second_factor, third_factor = jax.random.split(key, 3)
    head_scaling = jnp.exp(jax.random.uniform(third_factor, (KEY_VALUE_HEADS,), jnp.float32, math.log(0.4), math.log(1.6)))
    key_rows = jnp.clip(jax.random.normal(first_factor, (TOKEN_COUNT, KEY_VALUE_HEADS, HEAD_WIDTH), jnp.float32), -6.0, 6.0) * head_scaling[None, :, None]
    value_rows = jnp.clip(jax.random.normal(second_factor, (TOKEN_COUNT, KEY_VALUE_HEADS, HEAD_WIDTH), jnp.float32), -6.0, 6.0)
    pair_stacked = jnp.stack([key_rows.reshape(TOKEN_COUNT, KEY_VALUE_HEADS * HEAD_WIDTH), value_rows.reshape(TOKEN_COUNT, KEY_VALUE_HEADS * HEAD_WIDTH)], axis=1)
    return pair_stacked.astype(jnp.bfloat16)


def draw_span_mask(key, part):
    key = jax.random.fold_in(key, 3)
    lower = jax.random.randint(key, (N_SPAN, N_SPAN, FRAMES), 0, 2, jnp.int32)
    rows = jnp.arange(N_SPAN, dtype=jnp.int32)[:, None, None]
    cols = jnp.arange(N_SPAN, dtype=jnp.int32)[None, :, None]
    return jnp.where(rows == cols, 1, jnp.where(rows > cols, lower, 0)).astype(jnp.int32)


def touch_ends(entries, stream_key, least, top_value):
    longest = entries.shape.index(max(entries.shape))
    spots = []
    for shift in (0, 1):
        where = [jax.random.randint(jax.random.fold_in(stream_key, axis), (), 0, length) for axis, length in enumerate(entries.shape)]
        where[longest] = (where[longest] + shift) % entries.shape[longest]
        spots.append(tuple(where))
    return entries.at[spots[0]].set(least).at[spots[1]].set(top_value)


def level_of(stream_key, shape, pieces, least, largest):
    factor_of, own = 1.0, jax.random.fold_in(stream_key, 6)
    for position, shards_of in pieces:
        draws = jnp.exp(jax.random.uniform(jax.random.fold_in(own, position), (shards_of,), jnp.float32, least / len(pieces), largest / len(pieces)))
        factor_of = factor_of * jnp.repeat(draws, shape[position] // shards_of).reshape([-1 if axis == position else 1 for axis in range(len(shape))])
    return factor_of


def scatter_about(stream_key, dims, scale, reach, shards=(), kind=jnp.bfloat16):
    drawn = scale * jax.random.normal(stream_key, dims, jnp.float32)
    if shards:
        drawn = drawn * level_of(stream_key, dims, shards, -0.22, 0.18)
    return jnp.clip(drawn, -reach, reach).astype(kind)


def setup_inputs(seed: int = 0) -> dict:
    splits = jax.random.split(jax.random.key(seed), 9)
    return {
        "queries": draw_queries(jax.random.fold_in(splits[8], 71), 0),
        "key_value_pairs": draw_key_value_pairs(jax.random.fold_in(splits[8], 71), 0),
        "out_weight": scatter_about(splits[2], (QUERY_HEAD_COUNT * HEAD_WIDTH, D), (QUERY_HEAD_COUNT * HEAD_WIDTH) ** -0.5, 0.109375, ((0, 4), (1, 16))),
        "gate_table": scatter_about(splits[3], (LEVELS, D), 1.0, 4.0, ((1, 4),), jnp.float32),
        "norm_gain": jnp.clip(1.0 + 0.1 * jax.random.normal(splits[4], (D,), jnp.float32), 0.5, 1.5),
        "plan": jax.random.permutation(splits[5], N_SPAN).astype(jnp.int32),
        "noise_level": touch_ends(jax.random.randint(splits[6], (N_SPAN,), 0, LEVELS), jax.random.fold_in(splits[6], 1), 0, LEVELS - 1).astype(jnp.int32),
        "span_mask": draw_span_mask(jax.random.fold_in(splits[8], 71), 0),
    }


def reference(queries, key_value_pairs, out_weight, gate_table, norm_gain, plan, noise_level, span_mask):
    token_list = queries.shape[0]
    span_rows = token_list // N_SPAN
    frame_rows = span_rows // FRAMES
    heads_per_group = QUERY_HEAD_COUNT // KEY_VALUE_HEADS
    scale = 1.0 / math.sqrt(HEAD_WIDTH)
    visible = span_mask[plan[:, None], plan[None, :]]
    token_ids = jnp.arange(token_list, dtype=jnp.int32)
    key_group = (token_ids // span_rows).astype(jnp.int32)
    key_frame = (token_ids % span_rows // frame_rows).astype(jnp.int32)
    key_rows = key_value_pairs[:, 0].reshape(token_list, KEY_VALUE_HEADS, HEAD_WIDTH).astype(jnp.float32)
    value_rows = key_value_pairs[:, 1].reshape(token_list, KEY_VALUE_HEADS, HEAD_WIDTH).astype(jnp.float32)
    token_block = math.gcd(span_rows, 256)

    def attend_block(index):
        start = (index * token_block).astype(jnp.int32)
        query_rows = lax.dynamic_slice_in_dim(queries, start, token_block, 0)
        query_rows = query_rows.reshape(token_block, KEY_VALUE_HEADS, heads_per_group, HEAD_WIDTH).astype(jnp.float32)
        owner = start // span_rows
        seen = visible[owner][key_group, key_frame] > 0
        scores = jnp.einsum('tkgd,rkd->tkgr', query_rows, key_rows) * scale
        scores = jnp.where(seen, scores, -1e+30)
        peak = lax.optimization_barrier(jnp.max(scores, axis=-1, keepdims=True))
        weights = jnp.where(seen, jnp.exp(scores - peak), 0.0)
        total = lax.optimization_barrier(jnp.sum(weights, axis=-1))
        weights_low = lax.optimization_barrier(weights.astype(jnp.bfloat16)).astype(jnp.float32)
        mixed = jnp.einsum('tkgr,rkd->tkgd', weights_low, value_rows) / total[..., None]
        return mixed.reshape(token_block, QUERY_HEAD_COUNT * HEAD_WIDTH).astype(jnp.bfloat16)
    heads_out = lax.map(attend_block, jnp.arange(token_list // token_block, dtype=jnp.int32)).reshape(token_list, QUERY_HEAD_COUNT * HEAD_WIDTH)
    projected = jnp.dot(heads_out, out_weight, preferred_element_type=jnp.float32)
    power = lax.optimization_barrier(jnp.mean(projected * projected, axis=-1, keepdims=True))
    gate = gate_table[noise_level][key_group]
    return (projected * lax.rsqrt(power + 1e-06) * norm_gain * gate).astype(jnp.bfloat16)
```

```python
import functools
import math

import jax
import jax.numpy as jnp
from jax import lax
from jax.experimental import pallas as pl
from jax.experimental.pallas import tpu as pltpu
from jax.sharding import PartitionSpec as P

MESH = pl.DeviceIdType.MESH
F32, BF16 = jnp.float32, jnp.bfloat16
LOG2E = 1.4426950408889634
SCALE = LOG2E / math.sqrt(128)
NEAR = (1, -1, 2, -2)
FAR = (5, -5)
YS = (1, -1, 2)
XS = (2, 1, -1)
SLOTS = (0, 1, -1, 2, -2, 5, 6, 4, 7, 3, -5, -4, -6, -3, -7, 8)
GROUPS = ((0, 5), (5, 10), (10, 16))
NT = (((1,), (1,)), ((), ()))


def kernel(
    q_ref, kv_ref, w_ref, gate_ref, gain_ref, plan_ref, level_ref, mask_ref, out_ref,
    kvb, qs, kc, vc, acc, peak, part_s, part_r, lse_s, lse_r, heads, wb, ps, pr, pw_s, pw_r,
    ss, rs,
):
    span, seq, x = lax.axis_index("span"), lax.axis_index("seq"), lax.axis_index("tensor")
    core, z_hi = span % 2, span // 2
    z_lo, y = seq // 4, seq % 4
    z = z_hi * 4 + z_lo

    def dev(dx=0, dy=0, dz=0, flip=False):
        zz = (z + dz + 16) % 16
        cc = 1 - core if flip else core
        return ((zz // 4) * 2 + cc, (zz % 4) * 4 + (y + dy + 4) % 4, (x + dx + 4) % 4)

    barrier = pltpu.get_barrier_semaphore()
    partners = [dev(dz=d) for d in (1, -1, 2, -2, 3, -3, 5, -5)]
    partners += [dev(dy=d) for d in YS] + [dev(dx=d) for d in XS] + [dev(flip=True)]
    for p in partners:
        pl.semaphore_signal(barrier, inc=1, device_id=p, device_id_type=MESH)

    row = lax.broadcasted_iota(jnp.int32, (128, 128), 0)
    col = lax.broadcasted_iota(jnp.int32, (128, 128), 1)
    pick = jnp.where(col == 2 * (row % 64) + row // 64, 1.0, 0.0).astype(BF16)
    kvb[0, 0] = jnp.dot(pick, kv_ref[...], preferred_element_type=F32).astype(BF16)
    for h in range(6):
        qs[0, h * 64 : (h + 1) * 64, :] = q_ref[:, h * 128 : (h + 1) * 128]
    half = pl.multiple_of(core * 96, 16)
    rows_a = pl.ds(half, 48)
    rows_b = pl.ds(pl.multiple_of(half + 48, 16), 48)
    wb[z_lo, y, pl.ds(half, 96), :] = w_ref[pl.ds(half, 96), :]

    started = []

    def send(src, dst, to):
        i = len(started)
        c = pltpu.make_async_remote_copy(
            src_ref=src, dst_ref=dst, send_sem=ss.at[i], recv_sem=rs.at[i], device_id=to, device_id_type=MESH
        )
        c.start()
        started.append(c)
        return c

    def near(group):
        lo = GROUPS[group][0]
        return [send(kvb.at[0, lo], kvb.at[0, lo + 1 + i], dev(dz=-d)) for i, d in enumerate(NEAR)]

    def across(group):
        lo, hi = GROUPS[group]
        part = pl.ds(lo, hi - lo)
        return send(kvb.at[0, part], kvb.at[1, part], dev(flip=True))

    def arrived(copies):
        for c in copies:
            c.wait_recv()

    pl.semaphore_wait(barrier, len(partners))

    far = [send(kvb.at[0, 0], kvb.at[0, GROUPS[1 + i][0]], dev(dz=-d)) for i, d in enumerate(FAR)]
    near0 = near(0)
    q_in = [send(qs.at[0], qs.at[1 + i], dev(dy=-d)) for i, d in enumerate(YS)]
    w_b1 = [send(wb.at[z_lo, y, rows_b], wb.at[z_lo, y, rows_b], dev(dy=-d)) for d in YS]
    arrived(near0)
    across0 = across(0)
    arrived(far)
    near1, near2 = near(1), near(2)
    far_slot = GROUPS[1][0] + 5 * core
    eighth = send(kvb.at[0, far_slot], kvb.at[0, 15], dev(dz=6 * core - 3))
    far2 = 4 * core - 2
    z_to = (-1, 1, far2)
    w_a1 = [send(wb.at[z_lo, y, rows_a], wb.at[z_lo, y, rows_a], dev(dz=d)) for d in z_to]

    own_place = plan_ref[span]

    def ingest(group):
        lo, hi = GROUPS[group]
        own_k = kvb[0, 0, 0:64, :]
        i = 0
        for rc in (0, 1):
            for slot in range(lo, hi):
                zz = (z + SLOTS[slot] + 16) % 16
                there = (zz // 4) * 2 + (core if rc == 0 else 1 - core)
                seen = mask_ref[own_place, plan_ref[there], (zz % 4) * 4 + y] > 0
                at = slice(i * 64, (i + 1) * 64)
                kc[at, :] = jnp.where(seen, kvb[rc, slot, 0:64, :], own_k)
                vc[at, 0:128] = jnp.where(seen, kvb[rc, slot, 64:128, :], jnp.zeros((64, 128), BF16))
                vc[at, 128:256] = jnp.where(seen, jnp.ones((64, 128), BF16), jnp.zeros((64, 128), BF16))
                i += 1
        return i * 64

    def unit(k, keys, first):
        for r in range(0, 384, 128):
            rr = slice(r, r + 128)
            s = lax.dot_general(qs[k, rr, :], kc[0:keys, :], NT, preferred_element_type=F32)
            cols = [s[:, t : t + 128] for t in range(0, keys, 128)]
            top = functools.reduce(jnp.maximum, cols)
            top = jnp.broadcast_to(jnp.max(top, axis=1, keepdims=True) * SCALE, (128, 128))
            if not first:
                old = peak[k, rr, :]
                top = jnp.maximum(old, top)
            weights = jnp.concatenate([jnp.exp2(t * SCALE - top).astype(BF16) for t in cols], axis=1)
            added = jnp.dot(weights, vc[0:keys, :], preferred_element_type=F32)
            if first:
                acc[k, rr, :] = added
            else:
                fade = jnp.exp2(old - top)
                acc[k, rr, :] = acc[k, rr, :] * jnp.concatenate([fade, fade], axis=1) + added
            peak[k, rr, :] = top

    across0.wait_recv()
    keys = ingest(0)
    unit(0, keys, True)
    arrived(q_in)
    for k in (1, 2, 3):
        unit(k, keys, True)

    arrived(near1)
    across1 = across(1)
    arrived(w_b1)
    w_b2 = [send(wb.at[z_lo, :, rows_b], wb.at[z_lo, :, rows_b], dev(dz=d)) for d in z_to]
    w_sib = [send(wb.at[z_lo, :, rows_b], wb.at[z_lo, :, rows_b], dev(flip=True))]
    across1.wait_recv()
    keys = ingest(1)
    for k in range(4):
        unit(k, keys, False)

    arrived(near2)
    eighth.wait_recv()
    across2 = across(2)
    arrived(w_a1)
    w_a2 = [send(wb.at[:, y, rows_a], wb.at[:, y, rows_a], dev(dy=-d)) for d in YS]
    w_sib.append(send(wb.at[:, y, rows_a], wb.at[:, y, rows_a], dev(flip=True)))
    across2.wait_recv()
    keys = ingest(2)

    def finish(k):
        total = acc[k, :, 128:256]
        return acc[k, :, 0:128] / total, peak[k] + jnp.log(total) * LOG2E

    part_in = []
    for k in (3, 1, 2):
        unit(k, keys, False)
        mean, lse = finish(k)
        part_s[k - 1] = mean.astype(BF16)
        for t in range(3):
            lse_s[k - 1, :, t * 128 : (t + 1) * 128] = lse[t * 128 : (t + 1) * 128, :].T[0:8, :]
        to = dev(dy=YS[k - 1])
        part_in.append((k, send(part_s.at[k - 1], part_r.at[k - 1], to), send(lse_s.at[k - 1], lse_r.at[k - 1], to)))
    unit(0, keys, False)
    mean0, lse0 = finish(0)
    means, lses = [mean0], [lse0]
    for k, a, b in part_in:
        a.wait_recv()
        b.wait_recv()
        means.append(part_r[k - 1].astype(F32))
        lses.append(
            jnp.concatenate(
                [
                    jnp.broadcast_to(lse_r[k - 1, 0:1, t * 128 : (t + 1) * 128], (128, 128)).T
                    for t in range(3)
                ],
                axis=0,
            )
        )
    best = functools.reduce(jnp.maximum, lses)
    shares = [jnp.exp2(v - best) for v in lses]
    mixed = sum(m * s for m, s in zip(means, shares)) / sum(shares)
    mixed = mixed.astype(BF16)
    for h in range(6):
        heads[:, h * 128 : (h + 1) * 128] = mixed[h * 64 : (h + 1) * 64, :]

    for c, d in zip(w_b2, z_to):
        c.wait_recv()
        at = (z_lo - d + 4) % 4
        w_sib.append(send(wb.at[at, :, rows_b], wb.at[at, :, rows_b], dev(flip=True)))
    for c, d in zip(w_a2, YS):
        c.wait_recv()
        at = (y + d + 4) % 4
        w_sib.append(send(wb.at[:, at, rows_a], wb.at[:, at, rows_a], dev(flip=True)))
    arrived(w_sib)

    def project(to):
        return lax.dot_general(heads[...], wb[to].reshape(768, 768), NT, preferred_element_type=F32)

    sums_in = []
    for k, d in enumerate(XS):
        ps[k] = project((x + d + 4) % 4).astype(BF16)
        sums_in.append(send(ps.at[k], pr.at[k], dev(dx=d)))
    total = project(x)
    for k, c in enumerate(sums_in):
        c.wait_recv()
        total = total + pr[k].astype(F32)
    square = jnp.sum(total * total, axis=1, keepdims=True)
    square = jnp.concatenate([jnp.broadcast_to(square, (64, 128)), jnp.zeros((64, 128), F32)], axis=0)
    pw_s[...] = square.T[0:8, :]
    power_in = [send(pw_s, pw_r.at[k], dev(dx=d)) for k, d in enumerate(XS)]
    level = level_ref[span]
    levels = lax.broadcasted_iota(jnp.int32, gate_ref.shape, 0)
    gate = jnp.sum(jnp.where(levels == level, gate_ref[...], 0.0), axis=0, keepdims=True) * gain_ref[...]
    power = pw_s[...]
    for k, c in enumerate(power_in):
        c.wait_recv()
        power = power + pw_r[k]
    power = jnp.broadcast_to(power[0:1, :], (128, 128)).T[0:64, 0:1] * (1.0 / 3072)
    out_ref[...] = (total * lax.rsqrt(power + 1e-06) * gate).astype(BF16)
    for c in started:
        c.wait_send()


MESSAGES = 64


def local(queries, key_value_pairs, out_weight, gate_table, norm_gain, plan, noise_level, span_mask):
    vmem = pl.BlockSpec(memory_space=pltpu.VMEM)
    smem = pl.BlockSpec(memory_space=pltpu.SMEM)
    return pl.pallas_call(
        kernel,
        out_shape=jax.ShapeDtypeStruct((64, 768), BF16),
        in_specs=[vmem] * 5 + [smem] * 3,
        out_specs=vmem,
        scratch_shapes=[
            pltpu.VMEM((2, 16, 128, 128), BF16),
            pltpu.VMEM((4, 384, 128), BF16),
            pltpu.VMEM((768, 128), BF16),
            pltpu.VMEM((768, 256), BF16),
            pltpu.VMEM((4, 384, 256), F32),
            pltpu.VMEM((4, 384, 128), F32),
            pltpu.VMEM((3, 384, 128), BF16),
            pltpu.VMEM((3, 384, 128), BF16),
            pltpu.VMEM((3, 8, 384), F32),
            pltpu.VMEM((3, 8, 384), F32),
            pltpu.VMEM((64, 768), BF16),
            pltpu.VMEM((4, 4, 192, 768), BF16),
            pltpu.VMEM((3, 64, 768), BF16),
            pltpu.VMEM((3, 64, 768), BF16),
            pltpu.VMEM((8, 128), F32),
            pltpu.VMEM((3, 8, 128), F32),
            pltpu.SemaphoreType.DMA((MESSAGES,)),
            pltpu.SemaphoreType.DMA((MESSAGES,)),
        ],
        compiler_params=pltpu.CompilerParams(
            collective_id=0, has_side_effects=True, vmem_limit_bytes=48 * 2**20
        ),
    )(
        queries,
        key_value_pairs.reshape(128, 128),
        out_weight.T,
        gate_table,
        norm_gain.reshape(1, 768),
        plan,
        noise_level,
        span_mask,
    )


def solution(mesh):
    return jax.shard_map(
        local,
        mesh=mesh,
        in_specs=(
            P(("span", "seq"), "tensor"),
            P(("span", "seq"), None, "tensor"),
            P("tensor", "seq"),
            P(None, "tensor"),
            P("tensor"),
            P(),
            P(),
            P(),
        ),
        out_specs=P(("span", "seq"), "tensor"),
        check_vma=False,
    )
```

```python
import functools
import math

import jax
import jax.numpy as jnp
from jax import lax
from jax.experimental import pallas as pl
from jax.experimental.pallas import tpu as pltpu
from jax.sharding import PartitionSpec as P

MESH = pl.DeviceIdType.MESH
F32, BF16 = jnp.float32, jnp.bfloat16
LOG2E = 1.4426950408889634
SCALE = LOG2E / math.sqrt(128)
NEAR = (1, -1, 2, -2)
FAR = (5, -5)
YS = (1, -1, 2)
XS = (2, 1, -1)
SLOTS = (0, 1, -1, 2, -2, 5, 6, 4, 7, 3, -5, -4, -6, -3, -7, 8)
GROUPS = ((0, 5), (5, 10), (10, 16))
NT = (((1,), (1,)), ((), ()))


def kernel(
    q_hbm, kv_hbm, w_hbm, gate_hbm, gain_hbm, plan_hbm, level_hbm, mask_hbm, out_ref,
    q_ref, kv_ref, gate_ref, gain_ref, plan_ref, level_ref, mask_ref, ls, kvb, qs, kc, vc, acc, peak, part_s, part_r, lse_s, lse_r, heads, wb, ps, pr, pw_s, pw_r,
    ss, rs,
):
    span, seq, x = lax.axis_index("span"), lax.axis_index("seq"), lax.axis_index("tensor")
    core, z_hi = span % 2, span // 2
    z_lo, y = seq // 4, seq % 4
    z = z_hi * 4 + z_lo

    def dev(dx=0, dy=0, dz=0, flip=False):
        zz = (z + dz + 16) % 16
        cc = 1 - core if flip else core
        return ((zz // 4) * 2 + cc, (zz % 4) * 4 + (y + dy + 4) % 4, (x + dx + 4) % 4)

    barrier = pltpu.get_barrier_semaphore()
    partners = [dev(dz=d) for d in (1, -1, 2, -2, 3, -3, 5, -5)]
    partners += [dev(dy=d) for d in YS] + [dev(dx=d) for d in XS] + [dev(flip=True)]
    for p in partners:
        pl.semaphore_signal(barrier, inc=1, device_id=p, device_id_type=MESH)

    half = pl.multiple_of(core * 96, 16)
    rows_a, rows_b = pl.ds(0, 48), pl.ds(48, 48)
    loads = [
        pltpu.make_async_copy(src, dst, ls.at[i])
        for i, (src, dst) in enumerate(
            [
                (kv_hbm, kv_ref),
                (q_hbm, q_ref),
                (w_hbm.at[pl.ds(half, 96)], wb.at[z_lo, y]),
                (plan_hbm, plan_ref),
                (mask_hbm, mask_ref),
                (level_hbm, level_ref),
                (gate_hbm, gate_ref),
                (gain_hbm, gain_ref),
            ]
        )
    ]
    for c in loads:
        c.start()
    loads[0].wait()
    row = lax.broadcasted_iota(jnp.int32, (128, 128), 0)
    col = lax.broadcasted_iota(jnp.int32, (128, 128), 1)
    pick = jnp.where(col == 2 * (row % 64) + row // 64, 1.0, 0.0).astype(BF16)
    kvb[0, 0] = jnp.dot(pick, kv_ref[...], preferred_element_type=F32).astype(BF16)
    loads[1].wait()
    for h in range(6):
        qs[0, h * 64 : (h + 1) * 64, :] = q_ref[:, h * 128 : (h + 1) * 128]
    for c in loads[2:]:
        c.wait()

    started = []

    def send(src, dst, to):
        i = len(started)
        c = pltpu.make_async_remote_copy(
            src_ref=src, dst_ref=dst, send_sem=ss.at[i], recv_sem=rs.at[i], device_id=to, device_id_type=MESH
        )
        c.start()
        started.append(c)
        return c

    def near(group):
        lo = GROUPS[group][0]
        return [send(kvb.at[0, lo], kvb.at[0, lo + 1 + i], dev(dz=-d)) for i, d in enumerate(NEAR)]

    def across(group):
        lo, hi = GROUPS[group]
        part = pl.ds(lo, hi - lo)
        return send(kvb.at[0, part], kvb.at[1, part], dev(flip=True))

    def arrived(copies):
        for c in copies:
            c.wait_recv()

    pl.semaphore_wait(barrier, len(partners))

    far = [send(kvb.at[0, 0], kvb.at[0, GROUPS[1 + i][0]], dev(dz=-d)) for i, d in enumerate(FAR)]
    near0 = near(0)
    q_in = [send(qs.at[0], qs.at[1 + i], dev(dy=-d)) for i, d in enumerate(YS)]
    z_to = (-1, 1, 4 * core - 2)
    w_a1 = [send(wb.at[z_lo, y, rows_a], wb.at[z_lo, y, rows_a], dev(dz=d)) for d in z_to]
    w_b1 = [send(wb.at[z_lo, y, rows_b], wb.at[z_lo, y, rows_b], dev(dy=-d)) for d in YS]
    arrived(near0)
    across0 = across(0)
    arrived(far)
    near1, near2 = near(1), near(2)
    far_slot = GROUPS[1][0] + 5 * core
    eighth = send(kvb.at[0, far_slot], kvb.at[0, 15], dev(dz=6 * core - 3))
    arrived(w_a1)
    w_a2 = [send(wb.at[:, y, rows_a], wb.at[:, y, rows_a], dev(dy=-d)) for d in YS]

    own_place = plan_ref[span]

    def ingest(group):
        lo, hi = GROUPS[group]
        own_k = kvb[0, 0, 0:64, :]
        i = 0
        for rc in (0, 1):
            for slot in range(lo, hi):
                zz = (z + SLOTS[slot] + 16) % 16
                there = (zz // 4) * 2 + (core if rc == 0 else 1 - core)
                seen = mask_ref[own_place, plan_ref[there], (zz % 4) * 4 + y] > 0
                at = slice(i * 64, (i + 1) * 64)
                kc[at, :] = jnp.where(seen, kvb[rc, slot, 0:64, :], own_k)
                vc[at, 0:128] = jnp.where(seen, kvb[rc, slot, 64:128, :], jnp.zeros((64, 128), BF16))
                vc[at, 128:256] = jnp.where(seen, jnp.ones((64, 128), BF16), jnp.zeros((64, 128), BF16))
                i += 1
        return i * 64

    def unit(k, keys, first):
        for r in range(0, 384, 128):
            rr = slice(r, r + 128)
            s = lax.dot_general(qs[k, rr, :], kc[0:keys, :], NT, preferred_element_type=F32)
            cols = [s[:, t : t + 128] for t in range(0, keys, 128)]
            top = functools.reduce(jnp.maximum, cols)
            top = jnp.broadcast_to(jnp.max(top, axis=1, keepdims=True) * SCALE, (128, 128))
            if not first:
                old = peak[k, rr, :]
                top = jnp.maximum(old, top)
            weights = jnp.concatenate([jnp.exp2(t * SCALE - top).astype(BF16) for t in cols], axis=1)
            added = jnp.dot(weights, vc[0:keys, :], preferred_element_type=F32)
            if first:
                acc[k, rr, :] = added
            else:
                fade = jnp.exp2(old - top)
                acc[k, rr, :] = acc[k, rr, :] * jnp.concatenate([fade, fade], axis=1) + added
            peak[k, rr, :] = top

    across0.wait_recv()
    keys = ingest(0)
    unit(0, keys, True)
    arrived(q_in)
    for k in (1, 2, 3):
        unit(k, keys, True)

    arrived(w_b1)
    w_b2 = [send(wb.at[z_lo, :, rows_b], wb.at[z_lo, :, rows_b], dev(dz=d)) for d in z_to]
    arrived(near1)
    across1 = across(1)
    arrived(near2)
    eighth.wait_recv()
    across2 = across(2)
    across1.wait_recv()
    keys = ingest(1)
    for k in range(4):
        unit(k, keys, False)
    across2.wait_recv()
    keys = ingest(2)

    def finish(k):
        total = acc[k, :, 128:256]
        return acc[k, :, 0:128] / total, peak[k] + jnp.log(total) * LOG2E

    part_in = []
    for k in (3, 1, 2):
        unit(k, keys, False)
        mean, lse = finish(k)
        part_s[k - 1] = mean.astype(BF16)
        for t in range(3):
            lse_s[k - 1, :, t * 128 : (t + 1) * 128] = lse[t * 128 : (t + 1) * 128, :].T[0:8, :]
        to = dev(dy=YS[k - 1])
        part_in.append((k, send(part_s.at[k - 1], part_r.at[k - 1], to), send(lse_s.at[k - 1], lse_r.at[k - 1], to)))
    unit(0, keys, False)
    mean0, lse0 = finish(0)
    means, lses = [mean0], [lse0]
    for k, a, b in part_in:
        a.wait_recv()
        b.wait_recv()
        means.append(part_r[k - 1].astype(F32))
        lses.append(
            jnp.concatenate(
                [
                    jnp.broadcast_to(lse_r[k - 1, 0:1, t * 128 : (t + 1) * 128], (128, 128)).T
                    for t in range(3)
                ],
                axis=0,
            )
        )
    best = functools.reduce(jnp.maximum, lses)
    shares = [jnp.exp2(v - best) for v in lses]
    mixed = sum(m * s for m, s in zip(means, shares)) / sum(shares)
    mixed = mixed.astype(BF16)
    for h in range(6):
        heads[0:64, h * 128 : (h + 1) * 128] = mixed[h * 64 : (h + 1) * 64, :]
    heads_in = send(heads.at[pl.ds(0, 64)], heads.at[pl.ds(64, 64)], dev(flip=True))
    arrived(w_a2)
    arrived(w_b2)
    heads_in.wait_recv()

    def project(to):
        return lax.dot_general(heads[...], wb[to].reshape(384, 768), NT, preferred_element_type=F32)

    mine_in, other_in = [], []
    for k, d in enumerate(XS):
        ps[k] = project((x + d + 4) % 4).astype(BF16)
        own, sibling = pl.ds(0, 64), pl.ds(64, 64)
        mine_in.append(send(ps.at[k, own], pr.at[k, own], dev(dx=d)))
        other_in.append(send(ps.at[k, sibling], pr.at[k, sibling], dev(dx=d, flip=True)))
    last = project(x)
    ps[3, 64:128, :] = last[64:128, :].astype(BF16)
    other_in.append(send(ps.at[3, sibling], pr.at[3, sibling], dev(flip=True)))
    mine = last[0:64, :]
    for k, c in enumerate(mine_in):
        c.wait_recv()
        mine = mine + pr[k, 0:64, :].astype(F32)
    other = jnp.zeros((64, 384), F32)
    for k, c in enumerate(other_in):
        c.wait_recv()
        other = other + pr[k, 64:128, :].astype(F32)
    halves = (jnp.where(core == 0, mine, other), jnp.where(core == 0, other, mine))
    total = jnp.concatenate(
        [v[:, t * 96 : (t + 1) * 96] for t in range(4) for v in halves], axis=1
    )
    square = jnp.sum(total * total, axis=1, keepdims=True)
    square = jnp.concatenate([jnp.broadcast_to(square, (64, 128)), jnp.zeros((64, 128), F32)], axis=0)
    pw_s[...] = square.T[0:8, :]
    power_in = [send(pw_s, pw_r.at[k], dev(dx=d)) for k, d in enumerate(XS)]
    level = level_ref[span]
    levels = lax.broadcasted_iota(jnp.int32, gate_ref.shape, 0)
    gate = jnp.sum(jnp.where(levels == level, gate_ref[...], 0.0), axis=0, keepdims=True)
    power = pw_s[...]
    for k, c in enumerate(power_in):
        c.wait_recv()
        power = power + pw_r[k]
    power = jnp.broadcast_to(power[0:1, :], (128, 128)).T[0:64, 0:1] * (1.0 / 3072)
    total = total * lax.rsqrt(power + 1e-06)
    for t in range(6):
        at = slice(t * 128, (t + 1) * 128)
        out_ref[:, at] = (total[:, at] * (gain_ref[t : t + 1, :] * gate[:, at])).astype(BF16)
    for c in started:
        c.wait_send()


MESSAGES = 64


def local(queries, key_value_pairs, out_weight, gate_table, norm_gain, plan, noise_level, span_mask):
    hbm = pl.BlockSpec(memory_space=pltpu.HBM)
    return pl.pallas_call(
        kernel,
        out_shape=jax.ShapeDtypeStruct((64, 768), BF16),
        in_specs=[hbm] * 8,
        out_specs=pl.BlockSpec(memory_space=pltpu.VMEM),
        scratch_shapes=[
            pltpu.VMEM((64, 768), BF16),
            pltpu.VMEM((128, 128), BF16),
            pltpu.VMEM((64, 768), F32),
            pltpu.VMEM((6, 128), F32),
            pltpu.SMEM((8,), jnp.int32),
            pltpu.SMEM((8,), jnp.int32),
            pltpu.SMEM((8, 8, 16), jnp.int32),
            pltpu.SemaphoreType.DMA((8,)),
            pltpu.VMEM((2, 16, 128, 128), BF16),
            pltpu.VMEM((4, 384, 128), BF16),
            pltpu.VMEM((768, 128), BF16),
            pltpu.VMEM((768, 256), BF16),
            pltpu.VMEM((4, 384, 256), F32),
            pltpu.VMEM((4, 384, 128), F32),
            pltpu.VMEM((3, 384, 128), BF16),
            pltpu.VMEM((3, 384, 128), BF16),
            pltpu.VMEM((3, 8, 384), F32),
            pltpu.VMEM((3, 8, 384), F32),
            pltpu.VMEM((128, 768), BF16),
            pltpu.VMEM((4, 4, 96, 768), BF16),
            pltpu.VMEM((4, 128, 384), BF16),
            pltpu.VMEM((4, 128, 384), BF16),
            pltpu.VMEM((8, 128), F32),
            pltpu.VMEM((3, 8, 128), F32),
            pltpu.SemaphoreType.DMA((MESSAGES,)),
            pltpu.SemaphoreType.DMA((MESSAGES,)),
        ],
        compiler_params=pltpu.CompilerParams(
            collective_id=0, has_side_effects=True, vmem_limit_bytes=60 * 2**20
        ),
    )(
        queries,
        key_value_pairs.reshape(128, 128),
        out_weight.T,
        gate_table,
        norm_gain.reshape(6, 128),
        plan,
        noise_level,
        span_mask,
    )


def solution(mesh):
    return jax.shard_map(
        local,
        mesh=mesh,
        in_specs=(
            P(("span", "seq"), "tensor"),
            P(("span", "seq"), None, "tensor"),
            P("tensor", "seq"),
            P(None, "tensor"),
            P("tensor"),
            P(),
            P(),
            P(),
        ),
        out_specs=P(("span", "seq"), "tensor"),
        check_vma=False,
    )
```

```python
import functools
import math

import jax
import jax.numpy as jnp
from jax import lax
from jax.experimental import pallas as pl
from jax.experimental.pallas import tpu as pltpu
from jax.sharding import PartitionSpec as P

MESH = pl.DeviceIdType.MESH
F32, BF16 = jnp.float32, jnp.bfloat16
LOG2E = 1.4426950408889634
SCALE = LOG2E / math.sqrt(128)
YS = (1, -1, 2)
XS = (2, 1, -1)
SLOTS = (0, 1, -1, 3, -3, 2, 4, -2, -4, 6, -6, 5, 7, -5, -7, 8)
GROUPS = ((0, 4), (4, 10), (10, 16))
NT = (((1,), (1,)), ((), ()))


def kernel(
    q_hbm, kv_hbm, w_hbm, gate_hbm, gain_hbm, plan_hbm, level_hbm, mask_hbm, out_ref,
    q_ref, kv_ref, gate_ref, gain_ref, plan_ref, level_ref, mask_ref, ls, kvb, qs, kc, vc, acc, peak, part_s, part_r, lse_s, lse_r, heads, wb, ps, pr, pw_s, pw_r,
    ss, rs,
):
    span, seq, x = lax.axis_index("span"), lax.axis_index("seq"), lax.axis_index("tensor")
    core, z_hi = span % 2, span // 2
    z_lo, y = seq // 4, seq % 4
    z = z_hi * 4 + z_lo

    def dev(dx=0, dy=0, dz=0, flip=False):
        zz = (z + dz + 16) % 16
        cc = 1 - core if flip else core
        return ((zz // 4) * 2 + cc, (zz % 4) * 4 + (y + dy + 4) % 4, (x + dx + 4) % 4)

    barrier = pltpu.get_barrier_semaphore()
    partners = [dev(dz=d) for d in (1, -1, 2, -2, 3, -3)]
    partners += [dev(dy=d) for d in YS] + [dev(dx=d) for d in XS] + [dev(flip=True)]
    for p in partners:
        pl.semaphore_signal(barrier, inc=1, device_id=p, device_id_type=MESH)

    half = pl.multiple_of(core * 96, 16)
    rows_a, rows_b = pl.ds(0, 48), pl.ds(48, 48)
    loads = [
        pltpu.make_async_copy(src, dst, ls.at[i])
        for i, (src, dst) in enumerate(
            [
                (kv_hbm, kv_ref),
                (q_hbm, q_ref),
                (w_hbm.at[pl.ds(half, 96)], wb.at[0, 0]),
                (plan_hbm, plan_ref),
                (mask_hbm, mask_ref),
                (level_hbm, level_ref),
                (gate_hbm, gate_ref),
                (gain_hbm, gain_ref),
            ]
        )
    ]
    for c in loads:
        c.start()
    loads[0].wait()
    row = lax.broadcasted_iota(jnp.int32, (128, 128), 0)
    col = lax.broadcasted_iota(jnp.int32, (128, 128), 1)
    pick = jnp.where(col == 2 * (row % 64) + row // 64, 1.0, 0.0).astype(BF16)
    kvb[0, 0] = jnp.dot(pick, kv_ref[...], preferred_element_type=F32).astype(BF16)
    loads[1].wait()
    for h in range(6):
        qs[0, h * 64 : (h + 1) * 64, :] = q_ref[:, h * 128 : (h + 1) * 128]
    for c in loads[2:]:
        c.wait()

    started = []

    def send(src, dst, to):
        i = len(started)
        c = pltpu.make_async_remote_copy(
            src_ref=src, dst_ref=dst, send_sem=ss.at[i], recv_sem=rs.at[i], device_id=to, device_id_type=MESH
        )
        c.start()
        started.append(c)
        return c

    def pass_on(block, steps):
        src = kvb.at[0, SLOTS.index(block)]
        return [send(src, kvb.at[0, SLOTS.index(block - d)], dev(dz=d)) for d in steps]

    def across(group):
        lo, hi = GROUPS[group]
        part = pl.ds(lo, hi - lo)
        return send(kvb.at[0, part], kvb.at[1, part], dev(flip=True))

    def arrived(copies):
        for c in copies:
            c.wait_recv()

    pl.semaphore_wait(barrier, len(partners))

    z_to = (-1, 1, 4 * core - 2)
    far = pass_on(0, (-3, 3))
    w_a1 = [send(wb.at[0, 0, rows_a], wb.at[1 + i, 0, rows_a], dev(dz=d)) for i, d in enumerate(z_to)]
    near0 = pass_on(0, (-1, 1))
    w_b1 = [send(wb.at[0, 0, rows_b], wb.at[0, 1 + i, rows_b], dev(dy=-d)) for i, d in enumerate(YS)]
    q_in = [send(qs.at[0], qs.at[1 + i], dev(dy=-d)) for i, d in enumerate(YS)]
    w_a2 = [send(wb.at[0, 0, rows_a], wb.at[0, 1 + i, rows_a], dev(dy=-d)) for i, d in enumerate(YS)]
    arrived(far)
    relay = pass_on(3, (-3,)) + pass_on(-3, (3,))
    near1 = pass_on(3, (-1, 1)) + pass_on(-3, (1, -1))
    arrived(near0)
    across0 = across(0)
    arrived(w_a1)
    got = pl.ds(1, 3)
    w_a2 += [send(wb.at[got, 0, rows_a], wb.at[got, 1 + i, rows_a], dev(dy=-d)) for i, d in enumerate(YS)]
    arrived(relay)
    near2 = pass_on(6, (-1, 1)) + pass_on(-6, (1, -1))
    near2.append(send(kvb.at[0, SLOTS.index(6) + core], kvb.at[0, SLOTS.index(8)], dev(dz=4 * core - 2)))
    arrived(w_b1)
    w_b2 = [send(wb.at[0, :, rows_b], wb.at[1 + i, :, rows_b], dev(dz=d)) for i, d in enumerate(z_to)]
    arrived(near1)
    across1 = across(1)

    own_place = plan_ref[span]

    def ingest(group):
        lo, hi = GROUPS[group]
        own_k = kvb[0, 0, 0:64, :]
        i = 0
        for rc in (0, 1):
            for slot in range(lo, hi):
                zz = (z + SLOTS[slot] + 16) % 16
                there = (zz // 4) * 2 + (core if rc == 0 else 1 - core)
                seen = mask_ref[own_place, plan_ref[there], (zz % 4) * 4 + y] > 0
                at = slice(i * 64, (i + 1) * 64)
                kc[at, :] = jnp.where(seen, kvb[rc, slot, 0:64, :], own_k)
                vc[at, 0:128] = jnp.where(seen, kvb[rc, slot, 64:128, :], jnp.zeros((64, 128), BF16))
                vc[at, 128:256] = jnp.where(seen, jnp.ones((64, 128), BF16), jnp.zeros((64, 128), BF16))
                i += 1
        return i * 64

    def unit(k, keys, first):
        s = lax.dot_general(qs[k], kc[0:keys, :], NT, preferred_element_type=F32)
        cols = [s[:, t : t + 128] for t in range(0, keys, 128)]
        top = functools.reduce(jnp.maximum, cols)
        top = jnp.broadcast_to(jnp.max(top, axis=1, keepdims=True) * SCALE, (384, 128))
        if not first:
            old = peak[k]
            top = jnp.maximum(old, top)
        weights = jnp.concatenate([jnp.exp2(t * SCALE - top).astype(BF16) for t in cols], axis=1)
        added = jnp.dot(weights, vc[0:keys, :], preferred_element_type=F32)
        if first:
            acc[k] = added
        else:
            fade = jnp.exp2(old - top)
            acc[k] = acc[k] * jnp.concatenate([fade, fade], axis=1) + added
        peak[k] = top

    across0.wait_recv()
    keys = ingest(0)
    unit(0, keys, True)
    arrived(q_in)
    for k in (1, 2, 3):
        unit(k, keys, True)

    arrived(near2)
    across2 = across(2)
    across1.wait_recv()
    keys = ingest(1)
    for k in range(4):
        unit(k, keys, False)
    across2.wait_recv()
    keys = ingest(2)

    def finish(k):
        total = acc[k, :, 128:256]
        return acc[k, :, 0:128] / total, peak[k] + jnp.log(total) * LOG2E

    part_in = []
    for k in (3, 1, 2):
        unit(k, keys, False)
        mean, lse = finish(k)
        part_s[k - 1] = mean.astype(BF16)
        for t in range(3):
            lse_s[k - 1, :, t * 128 : (t + 1) * 128] = lse[t * 128 : (t + 1) * 128, :].T[0:8, :]
        to = dev(dy=YS[k - 1])
        part_in.append((k, send(part_s.at[k - 1], part_r.at[k - 1], to), send(lse_s.at[k - 1], lse_r.at[k - 1], to)))
    unit(0, keys, False)
    mean0, lse0 = finish(0)
    means, lses = [mean0], [lse0]
    for k, a, b in part_in:
        a.wait_recv()
        b.wait_recv()
        means.append(part_r[k - 1].astype(F32))
        lses.append(
            jnp.concatenate(
                [
                    jnp.broadcast_to(lse_r[k - 1, 0:1, t * 128 : (t + 1) * 128], (128, 128)).T
                    for t in range(3)
                ],
                axis=0,
            )
        )
    best = functools.reduce(jnp.maximum, lses)
    shares = [jnp.exp2(v - best) for v in lses]
    mixed = sum(m * s for m, s in zip(means, shares)) / sum(shares)
    mixed = mixed.astype(BF16)
    for h in range(6):
        heads[0:64, h * 128 : (h + 1) * 128] = mixed[h * 64 : (h + 1) * 64, :]
    heads_in = send(heads.at[pl.ds(0, 64)], heads.at[pl.ds(64, 64)], dev(flip=True))
    arrived(w_a2)
    arrived(w_b2)
    heads_in.wait_recv()

    def slot_of(to, here):
        d = (to - here + 4) % 4
        return jnp.where(d < 2, d, 5 - d)

    def project(to):
        w = jnp.concatenate([wb[slot_of(to, z_lo), slot_of(t, y)] for t in range(4)], axis=0)
        return lax.dot_general(heads[...], w, NT, preferred_element_type=F32)

    mine_in, other_in = [], []
    for k, d in enumerate(XS):
        ps[k] = project((x + d + 4) % 4).astype(BF16)
        own, sibling = pl.ds(0, 64), pl.ds(64, 64)
        mine_in.append(send(ps.at[k, own], pr.at[k, own], dev(dx=d)))
        other_in.append(send(ps.at[k, sibling], pr.at[k, sibling], dev(dx=d, flip=True)))
    last = project(x)
    ps[3, 64:128, :] = last[64:128, :].astype(BF16)
    other_in.append(send(ps.at[3, sibling], pr.at[3, sibling], dev(flip=True)))
    mine = last[0:64, :]
    for k, c in enumerate(mine_in):
        c.wait_recv()
        mine = mine + pr[k, 0:64, :].astype(F32)
    other = jnp.zeros((64, 384), F32)
    for k, c in enumerate(other_in):
        c.wait_recv()
        other = other + pr[k, 64:128, :].astype(F32)
    halves = (jnp.where(core == 0, mine, other), jnp.where(core == 0, other, mine))
    total = jnp.concatenate(
        [v[:, t * 96 : (t + 1) * 96] for t in range(4) for v in halves], axis=1
    )
    square = jnp.sum(total * total, axis=1, keepdims=True)
    square = jnp.concatenate([jnp.broadcast_to(square, (64, 128)), jnp.zeros((64, 128), F32)], axis=0)
    pw_s[...] = square.T[0:8, :]
    power_in = [send(pw_s, pw_r.at[k], dev(dx=d)) for k, d in enumerate(XS)]
    level = level_ref[span]
    levels = lax.broadcasted_iota(jnp.int32, gate_ref.shape, 0)
    gate = jnp.sum(jnp.where(levels == level, gate_ref[...], 0.0), axis=0, keepdims=True)
    power = pw_s[...]
    for k, c in enumerate(power_in):
        c.wait_recv()
        power = power + pw_r[k]
    power = jnp.broadcast_to(power[0:1, :], (128, 128)).T[0:64, 0:1] * (1.0 / 3072)
    total = total * lax.rsqrt(power + 1e-06)
    for t in range(6):
        at = slice(t * 128, (t + 1) * 128)
        out_ref[:, at] = (total[:, at] * (gain_ref[t : t + 1, :] * gate[:, at])).astype(BF16)
    for c in started:
        c.wait_send()


MESSAGES = 64


def local(queries, key_value_pairs, out_weight, gate_table, norm_gain, plan, noise_level, span_mask):
    hbm = pl.BlockSpec(memory_space=pltpu.HBM)
    return pl.pallas_call(
        kernel,
        out_shape=jax.ShapeDtypeStruct((64, 768), BF16),
        in_specs=[hbm] * 8,
        out_specs=pl.BlockSpec(memory_space=pltpu.VMEM),
        scratch_shapes=[
            pltpu.VMEM((64, 768), BF16),
            pltpu.VMEM((128, 128), BF16),
            pltpu.VMEM((64, 768), F32),
            pltpu.VMEM((6, 128), F32),
            pltpu.SMEM((8,), jnp.int32),
            pltpu.SMEM((8,), jnp.int32),
            pltpu.SMEM((8, 8, 16), jnp.int32),
            pltpu.SemaphoreType.DMA((8,)),
            pltpu.VMEM((2, 16, 128, 128), BF16),
            pltpu.VMEM((4, 384, 128), BF16),
            pltpu.VMEM((768, 128), BF16),
            pltpu.VMEM((768, 256), BF16),
            pltpu.VMEM((4, 384, 256), F32),
            pltpu.VMEM((4, 384, 128), F32),
            pltpu.VMEM((3, 384, 128), BF16),
            pltpu.VMEM((3, 384, 128), BF16),
            pltpu.VMEM((3, 8, 384), F32),
            pltpu.VMEM((3, 8, 384), F32),
            pltpu.VMEM((128, 768), BF16),
            pltpu.VMEM((4, 4, 96, 768), BF16),
            pltpu.VMEM((4, 128, 384), BF16),
            pltpu.VMEM((4, 128, 384), BF16),
            pltpu.VMEM((8, 128), F32),
            pltpu.VMEM((3, 8, 128), F32),
            pltpu.SemaphoreType.DMA((MESSAGES,)),
            pltpu.SemaphoreType.DMA((MESSAGES,)),
        ],
        compiler_params=pltpu.CompilerParams(
            collective_id=0, has_side_effects=True, vmem_limit_bytes=60 * 2**20
        ),
    )(
        queries,
        key_value_pairs.reshape(128, 128),
        out_weight.T,
        gate_table,
        norm_gain.reshape(6, 128),
        plan,
        noise_level,
        span_mask,
    )


def solution(mesh):
    return jax.shard_map(
        local,
        mesh=mesh,
        in_specs=(
            P(("span", "seq"), "tensor"),
            P(("span", "seq"), None, "tensor"),
            P("tensor", "seq"),
            P(None, "tensor"),
            P("tensor"),
            P(),
            P(),
            P(),
        ),
        out_specs=P(("span", "seq"), "tensor"),
        check_vma=False,
    )
```

```python
import functools
import math

import jax
import jax.numpy as jnp
from jax import lax
from jax.experimental import pallas as pl
from jax.experimental.pallas import tpu as pltpu
from jax.sharding import PartitionSpec as P

MESH = pl.DeviceIdType.MESH
F32, BF16 = jnp.float32, jnp.bfloat16
LOG2E = 1.4426950408889634
SCALE = LOG2E / math.sqrt(128)
YS = (1, -1, 2)
XS = (2, 1, -1)
SLOTS = (0, 1, -1, 3, -3, 2, 4, -2, -4, 6, -6, 5, 7, -5, -7, 8)
GROUPS = ((0, 4), (4, 10), (10, 16))
NT = (((1,), (1,)), ((), ()))


def kernel(
    q_hbm, kv_hbm, w_hbm, gate_hbm, gain_hbm, plan_hbm, level_hbm, mask_hbm, out_ref,
    q_ref, kv_ref, gate_ref, gain_ref, plan_ref, level_ref, mask_ref, ls, kvb, qs, kc, vc, acc, peak, part_s, part_r, lse_s, lse_r, heads, wb, ps, pr, pw_s, pw_r,
    ss, rs,
):
    span, seq, x = lax.axis_index("span"), lax.axis_index("seq"), lax.axis_index("tensor")
    core, z_hi = span % 2, span // 2
    z_lo, y = seq // 4, seq % 4
    z = z_hi * 4 + z_lo

    def dev(dx=0, dy=0, dz=0, flip=False):
        zz = (z + dz + 16) % 16
        cc = 1 - core if flip else core
        return ((zz // 4) * 2 + cc, (zz % 4) * 4 + (y + dy + 4) % 4, (x + dx + 4) % 4)

    barrier = pltpu.get_barrier_semaphore()
    partners = [dev(dz=d) for d in (1, -1, 2, -2, 3, -3)]
    partners += [dev(dy=d) for d in YS] + [dev(dx=d) for d in XS] + [dev(flip=True)]
    for p in partners:
        pl.semaphore_signal(barrier, inc=1, device_id=p, device_id_type=MESH)

    half = pl.multiple_of(core * 96, 16)
    rows_a, rows_b = pl.ds(0, 32), pl.ds(32, 64)
    loads = [
        pltpu.make_async_copy(src, dst, ls.at[i])
        for i, (src, dst) in enumerate(
            [
                (kv_hbm, kv_ref),
                (q_hbm, q_ref),
                (w_hbm.at[pl.ds(half, 96)], wb.at[0, 0]),
                (plan_hbm, plan_ref),
                (mask_hbm, mask_ref),
                (level_hbm, level_ref),
                (gate_hbm, gate_ref),
                (gain_hbm, gain_ref),
            ]
        )
    ]
    for c in loads:
        c.start()
    loads[0].wait()
    row = lax.broadcasted_iota(jnp.int32, (128, 128), 0)
    col = lax.broadcasted_iota(jnp.int32, (128, 128), 1)
    pick = jnp.where(col == 2 * (row % 64) + row // 64, 1.0, 0.0).astype(BF16)
    kvb[0, 0] = jnp.dot(pick, kv_ref[...], preferred_element_type=F32).astype(BF16)
    loads[1].wait()
    for h in range(6):
        qs[0, h * 64 : (h + 1) * 64, :] = q_ref[:, h * 128 : (h + 1) * 128]
    for c in loads[2:]:
        c.wait()

    started = []

    def send(src, dst, to):
        i = len(started)
        c = pltpu.make_async_remote_copy(
            src_ref=src, dst_ref=dst, send_sem=ss.at[i], recv_sem=rs.at[i], device_id=to, device_id_type=MESH
        )
        c.start()
        started.append(c)
        return c

    def pass_on(block, steps):
        src = kvb.at[0, SLOTS.index(block)]
        return [send(src, kvb.at[0, SLOTS.index(block - d)], dev(dz=d)) for d in steps]

    def across(group):
        lo, hi = GROUPS[group]
        part = pl.ds(lo, hi - lo)
        return send(kvb.at[0, part], kvb.at[1, part], dev(flip=True))

    def arrived(copies):
        for c in copies:
            c.wait_recv()

    pl.semaphore_wait(barrier, len(partners))

    z_to = (-1, 1, 4 * core - 2)
    far = pass_on(0, (-3, 3))
    w_a1 = [send(wb.at[0, 0, rows_a], wb.at[1 + i, 0, rows_a], dev(dz=d)) for i, d in enumerate(z_to)]
    near0 = pass_on(0, (-1, 1))
    q_in = [send(qs.at[0], qs.at[1 + i], dev(dy=-d)) for i, d in enumerate(YS)]
    w_b1 = [send(wb.at[0, 0, rows_b], wb.at[0, 1 + i, rows_b], dev(dy=-d)) for i, d in enumerate(YS)]
    arrived(far)
    relay = pass_on(3, (-3,)) + pass_on(-3, (3,))
    near1 = pass_on(3, (-1, 1)) + pass_on(-3, (1, -1))
    w_a2 = [send(wb.at[0, 0, rows_a], wb.at[0, 1 + i, rows_a], dev(dy=-d)) for i, d in enumerate(YS)]
    arrived(near0)
    across0 = across(0)
    arrived(w_a1)
    got = pl.ds(1, 3)
    w_a2 += [send(wb.at[got, 0, rows_a], wb.at[got, 1 + i, rows_a], dev(dy=-d)) for i, d in enumerate(YS)]
    arrived(relay)
    near2 = pass_on(6, (-1, 1)) + pass_on(-6, (1, -1))
    near2.append(send(kvb.at[0, SLOTS.index(6) + core], kvb.at[0, SLOTS.index(8)], dev(dz=4 * core - 2)))
    arrived(w_b1)
    w_b2 = [send(wb.at[0, :, rows_b], wb.at[1 + i, :, rows_b], dev(dz=d)) for i, d in enumerate((-1, 1))]
    arrived(near1)
    across1 = across(1)

    own_place = plan_ref[span]

    def ingest(group):
        lo, hi = GROUPS[group]
        own_k = kvb[0, 0, 0:64, :]
        i = 0
        for rc in (0, 1):
            for slot in range(lo, hi):
                zz = (z + SLOTS[slot] + 16) % 16
                there = (zz // 4) * 2 + (core if rc == 0 else 1 - core)
                seen = mask_ref[own_place, plan_ref[there], (zz % 4) * 4 + y] > 0
                at = slice(i * 64, (i + 1) * 64)
                kc[at, :] = jnp.where(seen, kvb[rc, slot, 0:64, :], own_k)
                vc[at, 0:128] = jnp.where(seen, kvb[rc, slot, 64:128, :], jnp.zeros((64, 128), BF16))
                vc[at, 128:256] = jnp.where(seen, jnp.ones((64, 128), BF16), jnp.zeros((64, 128), BF16))
                i += 1
        return i * 64

    def unit(k, keys, first):
        s = lax.dot_general(qs[k], kc[0:keys, :], NT, preferred_element_type=F32)
        cols = [s[:, t : t + 128] for t in range(0, keys, 128)]
        top = functools.reduce(jnp.maximum, cols)
        top = jnp.broadcast_to(jnp.max(top, axis=1, keepdims=True) * SCALE, (384, 128))
        if not first:
            old = peak[k]
            top = jnp.maximum(old, top)
        weights = jnp.concatenate([jnp.exp2(t * SCALE - top).astype(BF16) for t in cols], axis=1)
        added = jnp.dot(weights, vc[0:keys, :], preferred_element_type=F32)
        if first:
            acc[k] = added
        else:
            fade = jnp.exp2(old - top)
            acc[k] = acc[k] * jnp.concatenate([fade, fade], axis=1) + added
        peak[k] = top

    across0.wait_recv()
    keys = ingest(0)
    unit(0, keys, True)
    arrived(q_in)
    for k in (1, 2, 3):
        unit(k, keys, True)

    arrived(near2)
    across2 = across(2)
    across1.wait_recv()
    keys = ingest(1)
    for k in range(4):
        unit(k, keys, False)
    across2.wait_recv()
    keys = ingest(2)

    def finish(k):
        total = acc[k, :, 128:256]
        return acc[k, :, 0:128] / total, peak[k] + jnp.log(total) * LOG2E

    part_in = []
    for k in (3, 1, 2):
        unit(k, keys, False)
        mean, lse = finish(k)
        part_s[k - 1] = mean.astype(BF16)
        for t in range(3):
            lse_s[k - 1, :, t * 128 : (t + 1) * 128] = lse[t * 128 : (t + 1) * 128, :].T[0:8, :]
        to = dev(dy=YS[k - 1])
        part_in.append((k, send(part_s.at[k - 1], part_r.at[k - 1], to), send(lse_s.at[k - 1], lse_r.at[k - 1], to)))
    unit(0, keys, False)
    mean0, lse0 = finish(0)
    arrived(w_b2)
    low, high = pl.ds(0, 2), pl.ds(2, 2)
    w_b3 = [
        send(wb.at[1, low, rows_b], wb.at[3, low, rows_b], dev(dz=-1)),
        send(wb.at[2, high, rows_b], wb.at[3, high, rows_b], dev(dz=1)),
    ]
    means, lses = [mean0], [lse0]
    for k, a, b in part_in:
        a.wait_recv()
        b.wait_recv()
        means.append(part_r[k - 1].astype(F32))
        lses.append(
            jnp.concatenate(
                [
                    jnp.broadcast_to(lse_r[k - 1, 0:1, t * 128 : (t + 1) * 128], (128, 128)).T
                    for t in range(3)
                ],
                axis=0,
            )
        )
    best = functools.reduce(jnp.maximum, lses)
    shares = [jnp.exp2(v - best) for v in lses]
    mixed = sum(m * s for m, s in zip(means, shares)) / sum(shares)
    mixed = mixed.astype(BF16)
    for h in range(6):
        heads[0:64, h * 128 : (h + 1) * 128] = mixed[h * 64 : (h + 1) * 64, :]
    heads_in = send(heads.at[pl.ds(0, 64)], heads.at[pl.ds(64, 64)], dev(flip=True))
    arrived(w_a2)
    arrived(w_b3)
    heads_in.wait_recv()

    def slot_of(to, here):
        d = (to - here + 4) % 4
        return jnp.where(d < 2, d, 5 - d)

    def project(to):
        w = jnp.concatenate([wb[slot_of(to, z_lo), slot_of(t, y)] for t in range(4)], axis=0)
        return lax.dot_general(heads[...], w, NT, preferred_element_type=F32)

    mine_in, other_in = [], []
    for k, d in enumerate(XS):
        ps[k] = project((x + d + 4) % 4).astype(BF16)
        own, sibling = pl.ds(0, 64), pl.ds(64, 64)
        mine_in.append(send(ps.at[k, own], pr.at[k, own], dev(dx=d)))
        other_in.append(send(ps.at[k, sibling], pr.at[k, sibling], dev(dx=d, flip=True)))
    last = project(x)
    ps[3, 64:128, :] = last[64:128, :].astype(BF16)
    other_in.append(send(ps.at[3, sibling], pr.at[3, sibling], dev(flip=True)))
    mine = last[0:64, :]
    for k, c in enumerate(mine_in):
        c.wait_recv()
        mine = mine + pr[k, 0:64, :].astype(F32)
    other = jnp.zeros((64, 384), F32)
    for k, c in enumerate(other_in):
        c.wait_recv()
        other = other + pr[k, 64:128, :].astype(F32)
    halves = (jnp.where(core == 0, mine, other), jnp.where(core == 0, other, mine))
    total = jnp.concatenate(
        [v[:, t * 96 : (t + 1) * 96] for t in range(4) for v in halves], axis=1
    )
    square = jnp.sum(total * total, axis=1, keepdims=True)
    square = jnp.concatenate([jnp.broadcast_to(square, (64, 128)), jnp.zeros((64, 128), F32)], axis=0)
    pw_s[...] = square.T[0:8, :]
    power_in = [send(pw_s, pw_r.at[k], dev(dx=d)) for k, d in enumerate(XS)]
    level = level_ref[span]
    levels = lax.broadcasted_iota(jnp.int32, gate_ref.shape, 0)
    gate = jnp.sum(jnp.where(levels == level, gate_ref[...], 0.0), axis=0, keepdims=True)
    power = pw_s[...]
    for k, c in enumerate(power_in):
        c.wait_recv()
        power = power + pw_r[k]
    power = jnp.broadcast_to(power[0:1, :], (128, 128)).T[0:64, 0:1] * (1.0 / 3072)
    total = total * lax.rsqrt(power + 1e-06)
    for t in range(6):
        at = slice(t * 128, (t + 1) * 128)
        out_ref[:, at] = (total[:, at] * (gain_ref[t : t + 1, :] * gate[:, at])).astype(BF16)
    for c in started:
        c.wait_send()


MESSAGES = 64


def local(queries, key_value_pairs, out_weight, gate_table, norm_gain, plan, noise_level, span_mask):
    hbm = pl.BlockSpec(memory_space=pltpu.HBM)
    return pl.pallas_call(
        kernel,
        out_shape=jax.ShapeDtypeStruct((64, 768), BF16),
        in_specs=[hbm] * 8,
        out_specs=pl.BlockSpec(memory_space=pltpu.VMEM),
        scratch_shapes=[
            pltpu.VMEM((64, 768), BF16),
            pltpu.VMEM((128, 128), BF16),
            pltpu.VMEM((64, 768), F32),
            pltpu.VMEM((6, 128), F32),
            pltpu.SMEM((8,), jnp.int32),
            pltpu.SMEM((8,), jnp.int32),
            pltpu.SMEM((8, 8, 16), jnp.int32),
            pltpu.SemaphoreType.DMA((8,)),
            pltpu.VMEM((2, 16, 128, 128), BF16),
            pltpu.VMEM((4, 384, 128), BF16),
            pltpu.VMEM((768, 128), BF16),
            pltpu.VMEM((768, 256), BF16),
            pltpu.VMEM((4, 384, 256), F32),
            pltpu.VMEM((4, 384, 128), F32),
            pltpu.VMEM((3, 384, 128), BF16),
            pltpu.VMEM((3, 384, 128), BF16),
            pltpu.VMEM((3, 8, 384), F32),
            pltpu.VMEM((3, 8, 384), F32),
            pltpu.VMEM((128, 768), BF16),
            pltpu.VMEM((4, 4, 96, 768), BF16),
            pltpu.VMEM((4, 128, 384), BF16),
            pltpu.VMEM((4, 128, 384), BF16),
            pltpu.VMEM((8, 128), F32),
            pltpu.VMEM((3, 8, 128), F32),
            pltpu.SemaphoreType.DMA((MESSAGES,)),
            pltpu.SemaphoreType.DMA((MESSAGES,)),
        ],
        compiler_params=pltpu.CompilerParams(
            collective_id=0, has_side_effects=True, vmem_limit_bytes=60 * 2**20
        ),
    )(
        queries,
        key_value_pairs.reshape(128, 128),
        out_weight.T,
        gate_table,
        norm_gain.reshape(6, 128),
        plan,
        noise_level,
        span_mask,
    )


def solution(mesh):
    return jax.shard_map(
        local,
        mesh=mesh,
        in_specs=(
            P(("span", "seq"), "tensor"),
            P(("span", "seq"), None, "tensor"),
            P("tensor", "seq"),
            P(None, "tensor"),
            P("tensor"),
            P(),
            P(),
            P(),
        ),
        out_specs=P(("span", "seq"), "tensor"),
        check_vma=False,
    )
```

```python
import functools
import math

import jax
import jax.numpy as jnp
from jax import lax
from jax.experimental import pallas as pl
from jax.experimental.pallas import tpu as pltpu
from jax.sharding import PartitionSpec as P

MESH = pl.DeviceIdType.MESH
F32, BF16 = jnp.float32, jnp.bfloat16
LOG2E = 1.4426950408889634
SCALE = LOG2E / math.sqrt(128)
YS = (1, -1, 2)
XS = (2, 1, -1)
SLOTS = (0, 1, -1, 3, -3, 2, 4, -2, -4, 6, -6, 5, 7, -5, -7, 8)
GROUPS = ((0, 4), (4, 10), (10, 16))
NT = (((1,), (1,)), ((), ()))


def kernel(
    q_hbm, kv_hbm, w_hbm, gate_hbm, gain_hbm, plan_hbm, level_hbm, mask_hbm, out_ref,
    q_ref, kv_ref, gate_ref, gain_ref, plan_ref, level_ref, mask_ref, ls, kvb, qs, kc, vc, acc, peak, part_s, part_r, lse_s, lse_r, heads, wb, ps, pr, pw_s, pw_r,
    ss, rs,
):
    span, seq, x = lax.axis_index("span"), lax.axis_index("seq"), lax.axis_index("tensor")
    core, z_hi = span % 2, span // 2
    z_lo, y = seq // 4, seq % 4
    z = z_hi * 4 + z_lo

    def dev(dx=0, dy=0, dz=0, flip=False):
        zz = (z + dz + 16) % 16
        cc = 1 - core if flip else core
        return ((zz // 4) * 2 + cc, (zz % 4) * 4 + (y + dy + 4) % 4, (x + dx + 4) % 4)

    barrier = pltpu.get_barrier_semaphore()
    partners = [dev(dz=d) for d in (1, -1, 2, -2, 3, -3)]
    partners += [dev(dy=d) for d in YS] + [dev(dx=d) for d in XS] + [dev(flip=True)]
    for p in partners:
        pl.semaphore_signal(barrier, inc=1, device_id=p, device_id_type=MESH)

    half = pl.multiple_of(core * 96, 16)
    rows_a, rows_b = pl.ds(0, 32), pl.ds(32, 64)
    loads = [
        pltpu.make_async_copy(src, dst, ls.at[i])
        for i, (src, dst) in enumerate(
            [
                (kv_hbm, kv_ref),
                (q_hbm, q_ref),
                (w_hbm.at[pl.ds(half, 96)], wb.at[0, 0]),
                (plan_hbm, plan_ref),
                (mask_hbm, mask_ref),
                (level_hbm, level_ref),
                (gate_hbm, gate_ref),
                (gain_hbm, gain_ref),
            ]
        )
    ]
    for c in loads:
        c.start()
    loads[0].wait()
    row = lax.broadcasted_iota(jnp.int32, (128, 128), 0)
    col = lax.broadcasted_iota(jnp.int32, (128, 128), 1)
    pick = jnp.where(col == 2 * (row % 64) + row // 64, 1.0, 0.0).astype(BF16)
    kvb[0, 0] = jnp.dot(pick, kv_ref[...], preferred_element_type=F32).astype(BF16)
    loads[1].wait()
    for h in range(6):
        qs[0, h * 64 : (h + 1) * 64, :] = q_ref[:, h * 128 : (h + 1) * 128]
    for c in loads[2:]:
        c.wait()

    started = []

    def send(src, dst, to):
        i = len(started)
        c = pltpu.make_async_remote_copy(
            src_ref=src, dst_ref=dst, send_sem=ss.at[i], recv_sem=rs.at[i], device_id=to, device_id_type=MESH
        )
        c.start()
        started.append(c)
        return c

    def pass_on(block, steps):
        src = kvb.at[0, SLOTS.index(block)]
        return [send(src, kvb.at[0, SLOTS.index(block - d)], dev(dz=d)) for d in steps]

    def across(group):
        lo, hi = GROUPS[group]
        part = pl.ds(lo, hi - lo)
        return send(kvb.at[0, part], kvb.at[1, part], dev(flip=True))

    def arrived(copies):
        for c in copies:
            c.wait_recv()

    pl.semaphore_wait(barrier, len(partners))

    z_to = (-1, 1, 4 * core - 2)
    far = pass_on(0, (-3, 3))
    w_a1 = [send(wb.at[0, 0, rows_a], wb.at[1 + i, 0, rows_a], dev(dz=d)) for i, d in enumerate(z_to)]
    near0 = pass_on(0, (-1, 1))
    q_in = [send(qs.at[0], qs.at[1 + i], dev(dy=-d)) for i, d in enumerate(YS)]
    w_b1 = [send(wb.at[0, 0, rows_b], wb.at[0, 1 + i, rows_b], dev(dy=-d)) for i, d in enumerate(YS)]
    relay, near1 = [], []
    far[1].wait_recv()
    relay += pass_on(-3, (3,))
    near1 += pass_on(-3, (1, -1))
    far[0].wait_recv()
    relay += pass_on(3, (-3,))
    near1 += pass_on(3, (-1, 1))
    w_a2 = [send(wb.at[0, 0, rows_a], wb.at[0, 1 + i, rows_a], dev(dy=-d)) for i, d in enumerate(YS)]
    arrived(near0)
    across0 = across(0)
    arrived(w_a1)
    got = pl.ds(1, 3)
    w_a2 += [send(wb.at[got, 0, rows_a], wb.at[got, 1 + i, rows_a], dev(dy=-d)) for i, d in enumerate(YS)]
    near2 = []
    relay[0].wait_recv()
    near2 += pass_on(-6, (1, -1))
    relay[1].wait_recv()
    near2 += pass_on(6, (-1, 1))
    near2.append(send(kvb.at[0, SLOTS.index(6) + core], kvb.at[0, SLOTS.index(8)], dev(dz=4 * core - 2)))
    arrived(w_b1)
    w_b2 = [send(wb.at[0, :, rows_b], wb.at[1 + i, :, rows_b], dev(dz=d)) for i, d in enumerate((-1, 1))]
    arrived(near1)
    across1 = across(1)

    own_place = plan_ref[span]

    def ingest(group, sides=(0, 1)):
        lo, hi = GROUPS[group]
        own_k = kvb[0, 0, 0:64, :]
        i = 0
        for rc in sides:
            for slot in range(lo, hi):
                zz = (z + SLOTS[slot] + 16) % 16
                there = (zz // 4) * 2 + (core if rc == 0 else 1 - core)
                seen = mask_ref[own_place, plan_ref[there], (zz % 4) * 4 + y] > 0
                at = slice(i * 64, (i + 1) * 64)
                kc[at, :] = jnp.where(seen, kvb[rc, slot, 0:64, :], own_k)
                vc[at, 0:128] = jnp.where(seen, kvb[rc, slot, 64:128, :], jnp.zeros((64, 128), BF16))
                vc[at, 128:256] = jnp.where(seen, jnp.ones((64, 128), BF16), jnp.zeros((64, 128), BF16))
                i += 1
        return i * 64

    def unit(k, keys, first):
        s = lax.dot_general(qs[k], kc[0:keys, :], NT, preferred_element_type=F32)
        cols = [s[:, t : t + 128] for t in range(0, keys, 128)]
        top = functools.reduce(jnp.maximum, cols)
        top = jnp.broadcast_to(jnp.max(top, axis=1, keepdims=True) * SCALE, (384, 128))
        if not first:
            old = peak[k]
            top = jnp.maximum(old, top)
        weights = jnp.concatenate([jnp.exp2(t * SCALE - top).astype(BF16) for t in cols], axis=1)
        added = jnp.dot(weights, vc[0:keys, :], preferred_element_type=F32)
        if first:
            acc[k] = added
        else:
            fade = jnp.exp2(old - top)
            acc[k] = acc[k] * jnp.concatenate([fade, fade], axis=1) + added
        peak[k] = top

    across0.wait_recv()
    keys = ingest(0)
    unit(0, keys, True)
    arrived(q_in)
    for k in (1, 2, 3):
        unit(k, keys, True)

    arrived(near2)
    across2 = across(2)
    across1.wait_recv()
    keys = ingest(1)
    for k in range(4):
        unit(k, keys, False)
    keys = ingest(2, (0,))
    for k in range(4):
        unit(k, keys, False)
    across2.wait_recv()
    keys = ingest(2, (1,))

    def finish(k):
        total = acc[k, :, 128:256]
        return acc[k, :, 0:128] / total, peak[k] + jnp.log(total) * LOG2E

    part_in = []
    for k in (3, 1, 2):
        unit(k, keys, False)
        mean, lse = finish(k)
        part_s[k - 1] = mean.astype(BF16)
        for t in range(3):
            lse_s[k - 1, :, t * 128 : (t + 1) * 128] = lse[t * 128 : (t + 1) * 128, :].T[0:8, :]
        to = dev(dy=YS[k - 1])
        part_in.append((k, send(part_s.at[k - 1], part_r.at[k - 1], to), send(lse_s.at[k - 1], lse_r.at[k - 1], to)))
    unit(0, keys, False)
    mean0, lse0 = finish(0)
    arrived(w_b2)
    low, high = pl.ds(0, 2), pl.ds(2, 2)
    w_b3 = [
        send(wb.at[1, low, rows_b], wb.at[3, low, rows_b], dev(dz=-1)),
        send(wb.at[2, high, rows_b], wb.at[3, high, rows_b], dev(dz=1)),
    ]
    means, lses = [mean0], [lse0]
    for k, a, b in part_in:
        a.wait_recv()
        b.wait_recv()
        means.append(part_r[k - 1].astype(F32))
        lses.append(
            jnp.concatenate(
                [
                    jnp.broadcast_to(lse_r[k - 1, 0:1, t * 128 : (t + 1) * 128], (128, 128)).T
                    for t in range(3)
                ],
                axis=0,
            )
        )
    best = functools.reduce(jnp.maximum, lses)
    shares = [jnp.exp2(v - best) for v in lses]
    mixed = sum(m * s for m, s in zip(means, shares)) / sum(shares)
    mixed = mixed.astype(BF16)
    for h in range(6):
        heads[0:64, h * 128 : (h + 1) * 128] = mixed[h * 64 : (h + 1) * 64, :]
    heads_in = send(heads.at[pl.ds(0, 64)], heads.at[pl.ds(64, 64)], dev(flip=True))
    arrived(w_a2)
    arrived(w_b3)
    heads_in.wait_recv()

    def slot_of(to, here):
        d = (to - here + 4) % 4
        return jnp.where(d < 2, d, 5 - d)

    def project(to):
        w = jnp.concatenate([wb[slot_of(to, z_lo), slot_of(t, y)] for t in range(4)], axis=0)
        return lax.dot_general(heads[...], w, NT, preferred_element_type=F32)

    mine_in, other_in = [], []
    for k, d in enumerate(XS):
        ps[k] = project((x + d + 4) % 4).astype(BF16)
        own, sibling = pl.ds(0, 64), pl.ds(64, 64)
        mine_in.append(send(ps.at[k, own], pr.at[k, own], dev(dx=d)))
        other_in.append(send(ps.at[k, sibling], pr.at[k, sibling], dev(dx=d, flip=True)))
    last = project(x)
    ps[3, 64:128, :] = last[64:128, :].astype(BF16)
    other_in.append(send(ps.at[3, sibling], pr.at[3, sibling], dev(flip=True)))
    mine = last[0:64, :]
    for k, c in enumerate(mine_in):
        c.wait_recv()
        mine = mine + pr[k, 0:64, :].astype(F32)
    other = jnp.zeros((64, 384), F32)
    for k, c in enumerate(other_in):
        c.wait_recv()
        other = other + pr[k, 64:128, :].astype(F32)
    halves = (jnp.where(core == 0, mine, other), jnp.where(core == 0, other, mine))
    total = jnp.concatenate(
        [v[:, t * 96 : (t + 1) * 96] for t in range(4) for v in halves], axis=1
    )
    square = jnp.sum(total * total, axis=1, keepdims=True)
    square = jnp.concatenate([jnp.broadcast_to(square, (64, 128)), jnp.zeros((64, 128), F32)], axis=0)
    pw_s[...] = square.T[0:8, :]
    power_in = [send(pw_s, pw_r.at[k], dev(dx=d)) for k, d in enumerate(XS)]
    level = level_ref[span]
    levels = lax.broadcasted_iota(jnp.int32, gate_ref.shape, 0)
    gate = jnp.sum(jnp.where(levels == level, gate_ref[...], 0.0), axis=0, keepdims=True)
    power = pw_s[...]
    for k, c in enumerate(power_in):
        c.wait_recv()
        power = power + pw_r[k]
    power = jnp.broadcast_to(power[0:1, :], (128, 128)).T[0:64, 0:1] * (1.0 / 3072)
    total = total * lax.rsqrt(power + 1e-06)
    for t in range(6):
        at = slice(t * 128, (t + 1) * 128)
        out_ref[:, at] = (total[:, at] * (gain_ref[t : t + 1, :] * gate[:, at])).astype(BF16)
    for c in started:
        c.wait_send()


MESSAGES = 64


def local(queries, key_value_pairs, out_weight, gate_table, norm_gain, plan, noise_level, span_mask):
    hbm = pl.BlockSpec(memory_space=pltpu.HBM)
    return pl.pallas_call(
        kernel,
        out_shape=jax.ShapeDtypeStruct((64, 768), BF16),
        in_specs=[hbm] * 8,
        out_specs=pl.BlockSpec(memory_space=pltpu.VMEM),
        scratch_shapes=[
            pltpu.VMEM((64, 768), BF16),
            pltpu.VMEM((128, 128), BF16),
            pltpu.VMEM((64, 768), F32),
            pltpu.VMEM((6, 128), F32),
            pltpu.SMEM((8,), jnp.int32),
            pltpu.SMEM((8,), jnp.int32),
            pltpu.SMEM((8, 8, 16), jnp.int32),
            pltpu.SemaphoreType.DMA((8,)),
            pltpu.VMEM((2, 16, 128, 128), BF16),
            pltpu.VMEM((4, 384, 128), BF16),
            pltpu.VMEM((768, 128), BF16),
            pltpu.VMEM((768, 256), BF16),
            pltpu.VMEM((4, 384, 256), F32),
            pltpu.VMEM((4, 384, 128), F32),
            pltpu.VMEM((3, 384, 128), BF16),
            pltpu.VMEM((3, 384, 128), BF16),
            pltpu.VMEM((3, 8, 384), F32),
            pltpu.VMEM((3, 8, 384), F32),
            pltpu.VMEM((128, 768), BF16),
            pltpu.VMEM((4, 4, 96, 768), BF16),
            pltpu.VMEM((4, 128, 384), BF16),
            pltpu.VMEM((4, 128, 384), BF16),
            pltpu.VMEM((8, 128), F32),
            pltpu.VMEM((3, 8, 128), F32),
            pltpu.SemaphoreType.DMA((MESSAGES,)),
            pltpu.SemaphoreType.DMA((MESSAGES,)),
        ],
        compiler_params=pltpu.CompilerParams(
            collective_id=0, has_side_effects=True, vmem_limit_bytes=60 * 2**20
        ),
    )(
        queries,
        key_value_pairs.reshape(128, 128),
        out_weight.T,
        gate_table,
        norm_gain.reshape(6, 128),
        plan,
        noise_level,
        span_mask,
    )


def solution(mesh):
    return jax.shard_map(
        local,
        mesh=mesh,
        in_specs=(
            P(("span", "seq"), "tensor"),
            P(("span", "seq"), None, "tensor"),
            P("tensor", "seq"),
            P(None, "tensor"),
            P("tensor"),
            P(),
            P(),
            P(),
        ),
        out_specs=P(("span", "seq"), "tensor"),
        check_vma=False,
    )
```
